32 devices in a mesh: groups: 2 (over x), views: 16 (over z, y, core).
Axes of the slice: x: 2, y: 2, z: 4, core: 2. Of those that a mesh axis runs over, the one named last changes fastest.
Arguments:
- tokens: bfloat16 [32, 128, 1024], P(('groups', 'views')), parts along dimension 0, may hold values from -6 to 6
- in_gain: float32 [1024], replicated, may hold values from 0.7 to 6, as said below
- w_query: bfloat16 [1024, 1024], replicated, may hold values from -0.1875 to 0.1875
- w_key: bfloat16 [1024, 1024], replicated, may hold values from -0.1875 to 0.1875
- w_value: bfloat16 [1024, 1024], replicated, may hold values from -0.1875 to 0.1875
- w_out: bfloat16 [1024, 1024], replicated, may hold values from -0.1875 to 0.1875
- out_gain: float32 [1024], replicated, may hold values from 0.1 to 1.9
- covis_list: int32 [32, 12], P(('groups', 'views')), parts along dimension 0, may hold values from 0 to 15, as said below
- covis_count: int32 [32], P(('groups', 'views')), parts along dimension 0, may hold values from 2 to 12
Outputs:
- mixed: bfloat16 [32, 128, 1024], P(('groups', 'views')), parts along dimension 0
The draws below stay inside these ranges and needn't reach their ends.
There are 2 independent parts, one for each index of `groups`. The reference program is written for one: setup_inputs(seed, part) draws one part's arguments, and reference() takes and returns one part's arrays. A program takes and returns all parts, laid end to end along the dimension named above; an argument that names none is the same for every part. Nothing has to cross between parts.
Inputs may be any that keep to these rules, and one draw needn't show every extreme that they name: `covis_list`: row v lists 12 distinct view ids w, each with w - v modulo 16 among -6 to -1 and 1 to 6; only the first covis_count[v] entries are covisible views, the others are not used. `in_gain`: positive gains.
All inputs are finite; a program needn't handle non-finite values.
Results may differ from the reference program's by a relative error of at most 0.0085.
The reference program's roundings to bfloat16 on the way (of `normed`, `weights` and `head_normed`) count: a program that leaves them out, or rounds other values in their place, can miss the bound.
Values may be sent and summed in bfloat16 or wider, within the bound.
No kernel may reach another device: no remote copies, remote signals or barrier semaphores. Data moves between devices by JAX's collectives and lax.ppermute only.
A program may use at most 128 MiB of HBM per device.

```python
import jax
import jax.numpy as jnp
from jax import lax

D = 1024
HEADS = 16
HEAD_DIM = 64
TOK_VIEW = 128
REACH = 6
MAXCOV = 12
VIEWS = 16


def draw_in_gain(key, part):
    return jax.random.uniform(key, (D,), jnp.float32, 0.7, 1.3)


def covis_tables(key):
    base = jax.random.fold_in(key, 11)
    key_first, key_second, key_pick, key_other, key_order = jax.random.split(base, 5)
    span = 2 * REACH
    first = jax.random.randint(key_first, (VIEWS,), 0, span - 1)
    second = jax.random.randint(key_second, (VIEWS,), 0, span - 1)
    counts = 2 + first * second // (span - 2)
    pick = jax.random.randint(key_pick, (), 0, VIEWS)
    other = (pick + 1 + jax.random.randint(key_other, (), 0, VIEWS - 1)) % VIEWS
    counts = counts.at[pick].set(span).at[other].set(2)
    slot = jnp.arange(span, dtype=jnp.int32)
    offsets = jnp.where(slot < REACH, slot - REACH, slot - REACH + 1)
    ranking = jax.random.randint(key_order, (VIEWS, span), 0, 1 << 20) * span + slot[None, :]
    order = jnp.argsort(ranking, axis=1)
    chosen = offsets[order]
    ids = (jnp.arange(VIEWS, dtype=jnp.int32)[:, None] + chosen) % VIEWS
    return (ids.astype(jnp.int32), counts.astype(jnp.int32))


def draw_covis_list(key, part):
    return covis_tables(key)[0]


def draw_covis_count(key, part):
    return covis_tables(key)[1]


def level_of(rng, shape, shards, smallest, top_value):
    def one(position, parts):
        steps = jax.random.uniform(jax.random.fold_in(jax.random.fold_in(rng, 6), position), (parts,), jnp.float32, smallest / len(shards), top_value / len(shards))
        return jnp.repeat(jnp.exp(steps), shape[position] // parts).reshape((-1,) + (1,) * (len(shape) - position - 1))

    factor_of = one(*shards[0])
    for cut in shards[1:]:
        factor_of = factor_of * one(*cut)
    return factor_of


def gaussian(stream_key, extent, width, limit, cuts=(), held_as=jnp.bfloat16):
    loudness = level_of(stream_key, extent, cuts, -0.22, 0.18) if cuts else 1.0
    values = jax.random.normal(stream_key, extent, jnp.float32) * width * loudness
    return jnp.minimum(jnp.maximum(values, -limit), limit).astype(held_as)


def setup_inputs(seed: int = 0, part: int = 0) -> dict:
    arg_keys = jax.random.split(jax.random.key(seed), 10)
    part_keys = jax.random.split(jax.random.fold_in(arg_keys[9], part), 10)
    return {
        "tokens": gaussian(part_keys[0], (VIEWS, TOK_VIEW, D), 1.0, 6.0, ((0, 16),)),
        "in_gain": draw_in_gain(jax.random.fold_in(arg_keys[9], 71), part),
        "w_query": gaussian(arg_keys[2], (D, D), D ** -0.5, 0.1875),
        "w_key": gaussian(arg_keys[3], (D, D), D ** -0.5, 0.1875),
        "w_value": gaussian(arg_keys[4], (D, D), D ** -0.5, 0.1875),
        "w_out": gaussian(arg_keys[5], (D, D), D ** -0.5, 0.1875),
        "out_gain": jnp.clip(1.0 + 0.18 * jax.random.normal(arg_keys[6], (D,), jnp.float32), 0.1, 1.9),
        "covis_list": draw_covis_list(jax.random.fold_in(jax.random.fold_in(arg_keys[9], part), 71), part),
        "covis_count": draw_covis_count(jax.random.fold_in(jax.random.fold_in(arg_keys[9], part), 71), part),
    }


def rms_scale(values, gain):
    mean_sq = lax.optimization_barrier(jnp.mean(values * values, axis=-1, keepdims=True))
    return values * lax.rsqrt(mean_sq + 1e-06) * gain

def reference(tokens, in_gain, w_query, w_key, w_value, w_out, out_gain, covis_list, covis_count):
    normed = rms_scale(tokens.astype(jnp.float32), in_gain).astype(jnp.bfloat16)
    flat = normed.reshape(VIEWS * TOK_VIEW, D)
    query = jnp.dot(flat, w_query, preferred_element_type=jnp.float32).astype(jnp.bfloat16).reshape(VIEWS, TOK_VIEW, HEADS, HEAD_DIM)
    keys = jnp.dot(flat, w_key, preferred_element_type=jnp.float32).astype(jnp.bfloat16).reshape(VIEWS, TOK_VIEW, HEADS, HEAD_DIM)
    values = jnp.dot(flat, w_value, preferred_element_type=jnp.float32).astype(jnp.bfloat16).reshape(VIEWS, TOK_VIEW, HEADS, HEAD_DIM)
    offsets = jnp.arange(-REACH, REACH + 1, dtype=jnp.int32)
    slots = jnp.arange(MAXCOV, dtype=jnp.int32)
    scale = HEAD_DIM ** (-0.5)
    gain_heads = out_gain.reshape(HEADS, HEAD_DIM)

    def one_view(view):
        others = ((view + offsets) % VIEWS).astype(jnp.int32)
        valid = slots < covis_count[view]
        listed = jnp.any((covis_list[view][None, :] == others[:, None]) & valid[None, :], axis=1) | (offsets == 0)
        key_set = keys[others].reshape(-1, HEADS, HEAD_DIM).astype(jnp.float32)
        value_set = values[others].reshape(-1, HEADS, HEAD_DIM).astype(jnp.float32)
        scores = jnp.einsum('qhd,khd->qhk', query[view].astype(jnp.float32), key_set) * scale
        live = jnp.repeat(listed, TOK_VIEW)
        scores = jnp.where(live[None, None, :], scores, -jnp.inf)
        peak = lax.optimization_barrier(jnp.max(scores, axis=-1, keepdims=True))
        weights = jnp.exp(scores - peak)
        total = lax.optimization_barrier(jnp.sum(weights, axis=-1))
        numer = jnp.einsum('qhk,khd->qhd', weights.astype(jnp.bfloat16).astype(jnp.float32), value_set)
        attended = numer / total[..., None]
        head_normed = rms_scale(attended, gain_heads).astype(jnp.bfloat16).reshape(TOK_VIEW, D)
        update = jnp.dot(head_normed, w_out, preferred_element_type=jnp.float32)
        return (tokens[view].astype(jnp.float32) + update).astype(jnp.bfloat16)
    return lax.map(one_view, jnp.arange(VIEWS, dtype=jnp.int32))
```

```python
import functools

import jax
import jax.numpy as jnp
from jax import lax
from jax.experimental import pallas as pl
from jax.experimental.pallas import tpu as pltpu
from jax.sharding import PartitionSpec as P

HEADS = 16
HEAD_DIM = 64
REACH = 6
PAIRS = HEADS // 2
F32 = jnp.float32
BF16 = jnp.bfloat16
BY_ROWS = (((1,), (1,)), ((), ()))
BY_COLUMNS = (((0,), (0,)), ((), ()))
MIB = 1024 * 1024


def normalize(block, gain):
    values = block.astype(F32)
    mean_sq = jnp.mean(values * values, axis=-1, keepdims=True)
    return (values * lax.rsqrt(mean_sq + 1e-06) * gain).astype(BF16)


def project_query(normed, w_query, query_ref):
    query = jnp.dot(normed, w_query[...], preferred_element_type=F32).astype(BF16)
    query = query * jnp.asarray(HEAD_DIM**-0.5, BF16)
    rows = query.shape[0]
    lane = lax.broadcasted_iota(jnp.int32, (rows, 2 * HEAD_DIM), 1)
    for pair in range(PAIRS):
        both = query[:, 2 * HEAD_DIM * pair : 2 * HEAD_DIM * (pair + 1)]
        zero = jnp.zeros_like(both)
        query_ref[pair, :rows, :] = jnp.where(lane < HEAD_DIM, both, zero)
        query_ref[pair, rows:, :] = jnp.where(lane >= HEAD_DIM, both, zero)


def attend(normed, flags, w_key, w_value_t, query_ref, key_ref, value_ref, old, new):
    blocks = len(flags)
    rows = normed.shape[0] // blocks
    key_ref[...] = jnp.dot(normed, w_key[...], preferred_element_type=F32).astype(BF16)
    value_ref[...] = lax.dot_general(
        w_value_t[...], normed, BY_ROWS, preferred_element_type=F32
    ).astype(BF16)
    peak_ref, total_ref, numer_ref = new
    for pair in range(PAIRS):
        span = slice(2 * HEAD_DIM * pair, 2 * HEAD_DIM * (pair + 1))
        line = slice(pair, pair + 1)
        scores = lax.dot_general(
            key_ref[:, span], query_ref[pair], BY_ROWS, preferred_element_type=F32
        )
        parts = [scores[rows * b : rows * (b + 1)] for b in range(blocks)]
        peak = None if old is None else old[0][line, :]
        for flag, part in zip(flags, parts):
            top = jnp.max(part, axis=0, keepdims=True)
            if flag is not None:
                top = jnp.where(flag, top, -jnp.inf)
            peak = top if peak is None else jnp.maximum(peak, top)
        total = None
        weights = []
        for flag, part in zip(flags, parts):
            shift = peak if flag is None else jnp.where(flag, peak, jnp.inf)
            e = jnp.exp(part - shift)
            weights.append(e.astype(BF16))
            summed = jnp.sum(e, axis=0, keepdims=True)
            total = summed if total is None else total + summed
        weights = jnp.concatenate(weights, axis=0) if blocks > 1 else weights[0]
        numer = jnp.dot(value_ref[span, :], weights, preferred_element_type=F32)
        head_spans = [
            (slice(span.start + HEAD_DIM * j, span.start + HEAD_DIM * (j + 1)), slice(rows * j, rows * (j + 1)))
            for j in range(2)
        ]
        numers = [numer[HEAD_DIM * j : HEAD_DIM * (j + 1), head_spans[j][1]] for j in range(2)]
        if old is not None:
            keep = jnp.exp(old[0][line, :] - peak)
            total = old[1][line, :] * keep + total
            numers = [
                old[2][head, :] * keep[:, lanes] + part for (head, lanes), part in zip(head_spans, numers)
            ]
        peak_ref[line, :] = peak
        total_ref[line, :] = total
        for (head, _), part in zip(head_spans, numers):
            numer_ref[head, :] = part


def finish(total_ref, numer_ref, gain_col, w_out, source, headed_ref):
    rows = source.shape[0]
    for pair in range(PAIRS):
        for j in range(2):
            head = slice((2 * pair + j) * HEAD_DIM, (2 * pair + j + 1) * HEAD_DIM)
            attended = numer_ref[head, :] / total_ref[pair : pair + 1, rows * j : rows * (j + 1)]
            mean_sq = jnp.mean(attended * attended, axis=0, keepdims=True)
            headed_ref[head, :] = (attended * lax.rsqrt(mean_sq + 1e-06) * gain_col[head, :]).astype(BF16)
    update = lax.dot_general(headed_ref[...], w_out[...], BY_COLUMNS, preferred_element_type=F32)
    return (source.astype(F32) + update).astype(BF16)


def join_normed(block_refs, gain_ref):
    parts = [normalize(block[...], gain_ref[...]) for block in block_refs]
    return jnp.concatenate(parts, axis=0) if len(parts) > 1 else parts[0]


def first_kernel(slots, *refs):
    blocks = refs[: len(slots)]
    flags, in_gain, w_query, w_key, w_value_t, query, peak, total, numer, key, value = refs[len(slots) :]
    normed = join_normed(blocks, in_gain)
    project_query(normed[: blocks[0].shape[0]], w_query, query)
    on = [None] + [flags[s] > 0 for s in slots[1:]]
    attend(normed, on, w_key, w_value_t, query, key, value, None, (peak, total, numer))


def later_kernel(slots, *refs):
    blocks = refs[: len(slots)]
    flags, in_gain, w_key, w_value_t, query, peak, total, numer = refs[len(slots) : len(slots) + 8]
    new_peak, new_total, new_numer, key, value = refs[len(slots) + 8 :]
    on = [flags[s] > 0 for s in slots]
    attend(
        join_normed(blocks, in_gain), on, w_key, w_value_t, query, key, value,
        (peak, total, numer), (new_peak, new_total, new_numer),
    )


def last_kernel(slots, *refs):
    blocks = refs[: len(slots)]
    flags, in_gain, w_key, w_value_t, query, peak, total, numer = refs[len(slots) : len(slots) + 8]
    out_gain, w_out, source, out, new_peak, new_total, new_numer, headed, key, value = refs[len(slots) + 8 :]
    on = [flags[s] > 0 for s in slots]
    attend(
        join_normed(blocks, in_gain), on, w_key, w_value_t, query, key, value,
        (peak, total, numer), (new_peak, new_total, new_numer),
    )
    out[...] = finish(new_total, new_numer, out_gain, w_out, source[...], headed)


VMEM = pl.BlockSpec(memory_space=pltpu.VMEM)
SMEM = pl.BlockSpec(memory_space=pltpu.SMEM)


def scratch_for(blocks, rows, width):
    return [pltpu.VMEM((blocks * rows, width), BF16), pltpu.VMEM((width, blocks * rows), BF16)]


def cost_of(blocks, rows, width):
    keys = blocks * rows
    return pl.CostEstimate(
        flops=4 * keys * width * width + 8 * keys * rows * width,
        bytes_accessed=2 * keys * width + 4 * width * width,
        transcendentals=keys * rows * HEADS,
    )


def routes(axis, view_count):
    def swap(mask):
        return lambda block: lax.ppermute(block, axis, [(i, i ^ mask) for i in range(view_count)])

    def shift(step):
        return lambda block: lax.ppermute(
            block, axis, [(i, (i + step) % view_count) for i in range(view_count)]
        )

    masks = (0, 1, 2, 3, 4, 5, 6, 7, 10, 11, 12, 13, 14, 15)
    reached = all(
        any(v ^ mask == (v + d) % view_count for mask in masks)
        for v in range(view_count)
        for d in range(-REACH, REACH + 1)
    )
    if reached and max(masks) < view_count:

        def gather(own):
            got = {0: own}
            got[10] = swap(10)(own)
            got[2] = swap(2)(own)
            got[4] = swap(4)(own)
            got[1] = swap(1)(own)
            got[14] = swap(4)(got[10])
            got[12] = swap(6)(got[10])
            got[6] = swap(2)(got[4])
            for mask in (2, 4, 6, 10, 12, 14):
                got[mask ^ 1] = swap(1)(got[mask])
            return [got[mask] for mask in masks]

        return gather, lambda me: [me ^ mask for mask in masks]

    def gather(own):
        got = [own, swap(1)(own)]
        for step in (2, -2):
            moving = own
            for _ in range((REACH + 1) // 2):
                moving = shift(step)(moving)
                got += [moving, swap(1)(moving)]
        return got

    def owners(me):
        ids = [me, me ^ 1]
        for step in (2, -2):
            for hop in range(1, (REACH + 1) // 2 + 1):
                far = (me - step * hop) % view_count
                ids += [far, far ^ 1]
        return ids

    return gather, owners


CHUNKS = ((0, 1), (2, 3, 4, 5), (6, 7, 8, 9), (10, 11, 12, 13))


def on_device(view_count, tokens, in_gain, w_query, w_key, w_value, w_out, out_gain, covis_list, covis_count):
    source = tokens[0]
    rows, width = source.shape
    own_view = lax.axis_index("views")
    gather, owners = routes("views", view_count)
    blocks = gather(source)
    ids = jnp.stack(owners(own_view)).astype(jnp.int32)
    valid = jnp.arange(covis_list.shape[1], dtype=jnp.int32) < covis_count[0]
    flags = jnp.any((covis_list[0][None, :] == ids[:, None]) & valid[None, :], axis=1).astype(jnp.int32)
    gain_row = in_gain.reshape(1, width)
    gain_col = out_gain.reshape(width, 1)
    w_value_t = w_value.T
    pair_rows = 2 * rows
    state_shapes = [
        jax.ShapeDtypeStruct((PAIRS, pair_rows), F32),
        jax.ShapeDtypeStruct((PAIRS, pair_rows), F32),
        jax.ShapeDtypeStruct((width, rows), F32),
    ]
    state = None
    for index, slots in enumerate(CHUNKS):
        count = len(slots)
        parts = [blocks[s] for s in slots]
        params = pltpu.CompilerParams(vmem_limit_bytes=32 * MIB)
        cost = cost_of(count, rows, width)
        scratch = scratch_for(count, rows, width)
        if index == 0:
            query, *state = pl.pallas_call(
                functools.partial(first_kernel, slots),
                out_shape=[jax.ShapeDtypeStruct((PAIRS, pair_rows, 2 * HEAD_DIM), BF16)] + state_shapes,
                in_specs=[VMEM] * count + [SMEM] + [VMEM] * 4,
                out_specs=[VMEM] * 4,
                scratch_shapes=scratch,
                compiler_params=params,
                cost_estimate=cost,
            )(*parts, flags, gain_row, w_query, w_key, w_value_t)
        elif index < len(CHUNKS) - 1:
            state = pl.pallas_call(
                functools.partial(later_kernel, slots),
                out_shape=state_shapes,
                in_specs=[VMEM] * count + [SMEM] + [VMEM] * 7,
                out_specs=[VMEM] * 3,
                scratch_shapes=scratch,
                compiler_params=params,
                cost_estimate=cost,
            )(*parts, flags, gain_row, w_key, w_value_t, query, *state)
        else:
            mixed = pl.pallas_call(
                functools.partial(last_kernel, slots),
                out_shape=jax.ShapeDtypeStruct((rows, width), BF16),
                in_specs=[VMEM] * count + [SMEM] + [VMEM] * 10,
                out_specs=VMEM,
                scratch_shapes=[pltpu.VMEM(s.shape, s.dtype) for s in state_shapes]
                + [pltpu.VMEM((width, rows), BF16)]
                + scratch,
                compiler_params=params,
                cost_estimate=cost,
            )(*parts, flags, gain_row, w_key, w_value_t, query, *state, gain_col, w_out, source)
    return mixed[None]


def solution(mesh):
    in_specs = (
        P(("groups", "views"), None, None),
        P(),
        P(),
        P(),
        P(),
        P(),
        P(),
        P(("groups", "views"), None),
        P(("groups", "views")),
    )
    out_specs = P(("groups", "views"), None, None)
    return jax.shard_map(
        functools.partial(on_device, mesh.shape["views"]),
        mesh=mesh, in_specs=in_specs, out_specs=out_specs, check_vma=False,
    )
```

```python
import functools

import jax
import jax.numpy as jnp
from jax import lax
from jax.experimental import pallas as pl
from jax.experimental.pallas import tpu as pltpu
from jax.sharding import PartitionSpec as P

HEADS = 16
HEAD_DIM = 64
REACH = 6
PAIRS = HEADS // 2
F32 = jnp.float32
BF16 = jnp.bfloat16
BY_ROWS = (((1,), (1,)), ((), ()))
BY_COLUMNS = (((0,), (0,)), ((), ()))
MIB = 1024 * 1024


def normalize(block, gain):
    values = block.astype(F32)
    mean_sq = jnp.mean(values * values, axis=-1, keepdims=True)
    return (values * lax.rsqrt(mean_sq + 1e-06) * gain).astype(BF16)


def project_query(normed, w_query, query_ref):
    query = jnp.dot(normed, w_query[...], preferred_element_type=F32).astype(BF16)
    query = query * jnp.asarray(HEAD_DIM**-0.5, BF16)
    rows = query.shape[0]
    lane = lax.broadcasted_iota(jnp.int32, (rows, 2 * HEAD_DIM), 1)
    for pair in range(PAIRS):
        both = query[:, 2 * HEAD_DIM * pair : 2 * HEAD_DIM * (pair + 1)]
        zero = jnp.zeros_like(both)
        query_ref[pair, :rows, :] = jnp.where(lane < HEAD_DIM, both, zero)
        query_ref[pair, rows:, :] = jnp.where(lane >= HEAD_DIM, both, zero)


def attend(normed, flags, w_key, w_value_t, query_ref, key_ref, value_ref, old, new):
    blocks = len(flags)
    rows = normed.shape[0] // blocks
    peak_ref, total_ref, numer_ref = new

    def span_of(pair):
        return slice(2 * HEAD_DIM * pair, 2 * HEAD_DIM * (pair + 1))

    def scores_of(pair):
        return lax.dot_general(
            key_ref[:, span_of(pair)], query_ref[pair], BY_ROWS, preferred_element_type=F32
        )

    def soften(pair, scores):
        line = slice(pair, pair + 1)
        parts = [scores[rows * b : rows * (b + 1)] for b in range(blocks)]
        peak = None if old is None else old[0][line, :]
        for flag, part in zip(flags, parts):
            top = jnp.max(part, axis=0, keepdims=True)
            if flag is not None:
                top = jnp.where(flag, top, -jnp.inf)
            peak = top if peak is None else jnp.maximum(peak, top)
        total = None
        weights = []
        for flag, part in zip(flags, parts):
            shift = peak if flag is None else jnp.where(flag, peak, jnp.inf)
            e = jnp.exp(part - shift)
            weights.append(e.astype(BF16))
            summed = jnp.sum(e, axis=0, keepdims=True)
            total = summed if total is None else total + summed
        keep = None
        if old is not None:
            keep = jnp.exp(old[0][line, :] - peak)
            total = old[1][line, :] * keep + total
        peak_ref[line, :] = peak
        total_ref[line, :] = total
        return (jnp.concatenate(weights, axis=0) if blocks > 1 else weights[0]), keep

    def gather_values(pair, weights, keep):
        span = span_of(pair)
        numer = jnp.dot(value_ref[span, :], weights, preferred_element_type=F32)
        for j in range(2):
            head = slice(span.start + HEAD_DIM * j, span.start + HEAD_DIM * (j + 1))
            lanes = slice(rows * j, rows * (j + 1))
            part = numer[HEAD_DIM * j : HEAD_DIM * (j + 1), lanes]
            if keep is not None:
                part = old[2][head, :] * keep[:, lanes] + part
            numer_ref[head, :] = part

    key_ref[...] = jnp.dot(normed, w_key[...], preferred_element_type=F32).astype(BF16)
    scores = scores_of(0)
    value_ref[...] = lax.dot_general(
        w_value_t[...], normed, BY_ROWS, preferred_element_type=F32
    ).astype(BF16)
    held = None
    for pair in range(PAIRS):
        ahead = scores_of(pair + 1) if pair + 1 < PAIRS else None
        if held is not None:
            gather_values(pair - 1, *held)
        held = soften(pair, scores)
        scores = ahead
    gather_values(PAIRS - 1, *held)


def finish(total_ref, numer_ref, gain_col, w_out, source, headed_ref):
    rows = source.shape[0]
    for pair in range(PAIRS):
        for j in range(2):
            head = slice((2 * pair + j) * HEAD_DIM, (2 * pair + j + 1) * HEAD_DIM)
            attended = numer_ref[head, :] / total_ref[pair : pair + 1, rows * j : rows * (j + 1)]
            mean_sq = jnp.mean(attended * attended, axis=0, keepdims=True)
            headed_ref[head, :] = (attended * lax.rsqrt(mean_sq + 1e-06) * gain_col[head, :]).astype(BF16)
    update = lax.dot_general(headed_ref[...], w_out[...], BY_COLUMNS, preferred_element_type=F32)
    return (source.astype(F32) + update).astype(BF16)


def join_normed(block_refs, gain_ref):
    parts = [normalize(block[...], gain_ref[...]) for block in block_refs]
    return jnp.concatenate(parts, axis=0) if len(parts) > 1 else parts[0]


def listed(owners, slots, covis_list, covis_count):
    ids = owners(lax.axis_index("views"))
    count = covis_count[0]
    entries = [jnp.where(i < count, covis_list[0, i], -1) for i in range(covis_list.shape[1])]
    return [functools.reduce(jnp.logical_or, [entry == ids[s] for entry in entries]) for s in slots]


def first_kernel(
    owners, slots, own, other, covis_list, covis_count, in_gain, w_query, w_key, w_value,
    query, peak, total, numer, w_key_here, w_value_t,
    own_here, in_gain_here, w_query_here, w_value_here, key, value, arrived,
):
    copies = [
        pltpu.make_async_copy(source, target, arrived.at[i])
        for i, (source, target) in enumerate(
            (
                (own, own_here),
                (in_gain, in_gain_here),
                (w_query, w_query_here),
                (w_value, w_value_here),
                (w_key, w_key_here),
            )
        )
    ]
    for copy in copies:
        copy.start()
    flags = [None] + listed(owners, slots, covis_list, covis_count)
    copies[0].wait()
    copies[1].wait()
    normed = join_normed((own_here, other), in_gain_here)
    copies[2].wait()
    project_query(normed[: own.shape[0]], w_query_here, query)
    copies[3].wait()
    w_value_t[...] = w_value_here[...].T
    copies[4].wait()
    attend(normed, flags, w_key_here, w_value_t, query, key, value, None, (peak, total, numer))


def later_kernel(slots, owners, *refs):
    blocks = refs[: len(slots)]
    covis_list, covis_count, in_gain, w_key, w_value_t, query, peak, total, numer = refs[len(slots) : len(slots) + 9]
    new_peak, new_total, new_numer, key, value = refs[len(slots) + 9 :]
    attend(
        join_normed(blocks, in_gain), listed(owners, slots, covis_list, covis_count),
        w_key, w_value_t, query, key, value,
        (peak, total, numer), (new_peak, new_total, new_numer),
    )


def last_kernel(slots, owners, *refs):
    blocks = refs[: len(slots)]
    covis_list, covis_count, in_gain, w_key, w_value_t, query, peak, total, numer = refs[len(slots) : len(slots) + 9]
    out_gain, w_out, source, out = refs[len(slots) + 9 : len(slots) + 13]
    new_peak, new_total, new_numer, headed, w_out_here, source_here, arrived, key, value = refs[len(slots) + 13 :]
    copies = [
        pltpu.make_async_copy(w_out, w_out_here, arrived.at[0]),
        pltpu.make_async_copy(source, source_here, arrived.at[1]),
    ]
    for copy in copies:
        copy.start()
    attend(
        join_normed(blocks, in_gain), listed(owners, slots, covis_list, covis_count),
        w_key, w_value_t, query, key, value,
        (peak, total, numer), (new_peak, new_total, new_numer),
    )
    for copy in copies:
        copy.wait()
    out[...] = finish(new_total, new_numer, out_gain, w_out_here, source_here[...], headed)


VMEM = pl.BlockSpec(memory_space=pltpu.VMEM)
SMEM = pl.BlockSpec(memory_space=pltpu.SMEM)
HBM = pl.BlockSpec(memory_space=pltpu.HBM)


def scratch_for(blocks, rows, width):
    return [pltpu.VMEM((blocks * rows, width), BF16), pltpu.VMEM((width, blocks * rows), BF16)]


def in_hbm(array):
    return pltpu.with_memory_space_constraint(array, pltpu.HBM)


def tie(block, *done):
    return lax.optimization_barrier((block, *done))[0]


def routes(axis, view_count):
    def swap(mask):
        return lambda block: lax.ppermute(block, axis, [(i, i ^ mask) for i in range(view_count)])

    def shift(step):
        return lambda block: lax.ppermute(
            block, axis, [(i, (i + step) % view_count) for i in range(view_count)]
        )

    masks = (1, 2, 4, 10, 3, 5, 6, 11, 7, 12, 14, 13, 15)
    reached = all(
        v == (v + d) % view_count or any(v ^ mask == (v + d) % view_count for mask in masks)
        for v in range(view_count)
        for d in range(-REACH, REACH + 1)
    )
    if reached and max(masks) < view_count:

        def first(own):
            return {mask: swap(mask)(own) for mask in (10, 4, 2, 1)}

        def second(got, after):
            got[12] = swap(6)(after(got[10]))
            got[14] = swap(4)(after(got[10]))
            got[6] = swap(2)(after(got[4]))
            for mask in (2, 4):
                got[mask ^ 1] = swap(1)(after(got[mask]))

        def third(got, after):
            for mask in (6, 10):
                got[mask ^ 1] = swap(1)(after(got[mask]))

        def fourth(got, after):
            for mask in (12, 14):
                got[mask ^ 1] = swap(1)(after(got[mask]))

        return first, second, third, fourth, masks, lambda me: {mask: me ^ mask for mask in masks}

    hops = (REACH + 1) // 2
    names = ["partner"] + [(way, hop, side) for hop in range(1, hops + 1) for side in (0, 1) for way in (2, -2)]

    def first(own):
        got = {"partner": swap(1)(own)}
        for way in (2, -2):
            got[way, 1, 0] = shift(way)(own)
        return got

    def second(got, after):
        for way in (2, -2):
            for hop in range(2, hops + 1):
                got[way, hop, 0] = shift(way)(after(got[way, hop - 1, 0]))
            got[way, 1, 1] = swap(1)(after(got[way, 1, 0]))

    def third(got, after):
        for way in (2, -2):
            got[way, 2, 1] = swap(1)(after(got[way, 2, 0]))

    def fourth(got, after):
        for way in (2, -2):
            for hop in range(3, hops + 1):
                got[way, hop, 1] = swap(1)(after(got[way, hop, 0]))

    def owners(me):
        ids = {"partner": me ^ 1}
        for way in (2, -2):
            for hop in range(1, hops + 1):
                far = lax.rem(me - way * hop + view_count, view_count)
                ids[way, hop, 0] = far
                ids[way, hop, 1] = far ^ 1
        return ids

    return first, second, third, fourth, names, owners


def cost_of(blocks, rows, width):
    keys = blocks * rows
    return pl.CostEstimate(
        flops=3 * (4 * keys * width * width + 8 * keys * rows * width),
        bytes_accessed=2 * keys * width,
        transcendentals=keys * rows * HEADS,
    )


def on_device(view_count, tokens, in_gain, w_query, w_key, w_value, w_out, out_gain, covis_list, covis_count):
    source = tokens[0]
    rows, width = source.shape
    first, second, third, fourth, names, owners = routes("views", view_count)
    gain_row = in_gain.reshape(1, width)
    gain_col = out_gain.reshape(width, 1)
    pair_rows = 2 * rows
    state_shapes = [
        pltpu.VMEM((PAIRS, pair_rows), F32),
        pltpu.VMEM((PAIRS, pair_rows), F32),
        pltpu.VMEM((width, rows), F32),
    ]
    params = pltpu.CompilerParams(vmem_limit_bytes=24 * MIB)

    def call_later(got, slots, state, tail=None):
        count = len(slots)
        held = [
            pltpu.with_memory_space_constraint(x, pltpu.VMEM) for x in (w_key_here, w_value_t, query, *state)
        ]
        parts = [got[s] for s in slots] + [covis_list, covis_count, gain_row] + held
        specs = [VMEM] * count + [SMEM] * 2 + [VMEM] * 7
        scratch = scratch_for(count, rows, width)
        if tail is None:
            return pl.pallas_call(
                functools.partial(later_kernel, slots, owners),
                out_shape=state_shapes,
                in_specs=specs,
                out_specs=[VMEM] * 3,
                scratch_shapes=scratch,
                compiler_params=params,
                cost_estimate=cost_of(count, rows, width),
            )(*parts)
        return pl.pallas_call(
            functools.partial(last_kernel, slots, owners),
            out_shape=jax.ShapeDtypeStruct((rows, width), BF16),
            in_specs=specs + [VMEM, HBM, HBM],
            out_specs=VMEM,
            scratch_shapes=state_shapes
            + [pltpu.VMEM((width, rows), BF16), pltpu.VMEM(w_out.shape, BF16)]
            + [pltpu.VMEM(source.shape, BF16), pltpu.SemaphoreType.DMA((2,))]
            + scratch,
            compiler_params=params,
            cost_estimate=cost_of(count, rows, width),
        )(*parts, *tail)

    got = first(source)
    query, *state, w_key_here, w_value_t = pl.pallas_call(
        functools.partial(first_kernel, owners, names[:1]),
        out_shape=[pltpu.VMEM((PAIRS, pair_rows, 2 * HEAD_DIM), BF16)]
        + state_shapes
        + [pltpu.VMEM(w_key.shape, BF16), pltpu.VMEM(w_value.shape, BF16)],
        in_specs=[HBM, VMEM, SMEM, SMEM, HBM, HBM, HBM, HBM],
        out_specs=[VMEM] * 6,
        scratch_shapes=[
            pltpu.VMEM(source.shape, BF16),
            pltpu.VMEM(gain_row.shape, F32),
            pltpu.VMEM(w_query.shape, BF16),
            pltpu.VMEM(w_value.shape, BF16),
        ]
        + scratch_for(2, rows, width)
        + [pltpu.SemaphoreType.DMA((5,))],
        compiler_params=params,
        cost_estimate=cost_of(2, rows, width),
    )(
        in_hbm(source), got[names[0]], covis_list, covis_count,
        *map(in_hbm, (gain_row, w_query, w_key, w_value)),
    )
    mark = state[0]
    second(got, lambda block: tie(block, mark))
    state = call_later(got, names[1:4], state)
    third(got, lambda block: tie(block, state[0]))
    state = call_later(got, names[4:7], state)
    fourth(got, lambda block: tie(block, state[0]))
    state = call_later(got, names[7:11], state)
    return call_later(got, names[11:], state, (gain_col, in_hbm(w_out), in_hbm(source)))[None]


def solution(mesh):
    in_specs = (
        P(("groups", "views"), None, None),
        P(),
        P(),
        P(),
        P(),
        P(),
        P(),
        P(("groups", "views"), None),
        P(("groups", "views")),
    )
    out_specs = P(("groups", "views"), None, None)
    return jax.shard_map(
        functools.partial(on_device, mesh.shape["views"]),
        mesh=mesh, in_specs=in_specs, out_specs=out_specs, check_vma=False,
    )
```

```python
import functools

import jax
import jax.numpy as jnp
from jax import lax
from jax.experimental import pallas as pl
from jax.experimental.pallas import tpu as pltpu
from jax.sharding import PartitionSpec as P

HEADS = 16
HEAD_DIM = 64
REACH = 6
PAIRS = HEADS // 2
GROUP = 2
WEIGHT = (3, 3, 3, 3, 3, 3)
F32 = jnp.float32
BF16 = jnp.bfloat16
BY_ROWS = (((1,), (1,)), ((), ()))
BY_COLUMNS = (((0,), (0,)), ((), ()))
MIB = 1024 * 1024


def normalize(block, gain):
    values = block.astype(F32)
    mean_sq = jnp.mean(values * values, axis=-1, keepdims=True)
    return (values * lax.rsqrt(mean_sq + 1e-06) * gain).astype(BF16)


def project_query(normed, w_query, query_ref):
    query = jnp.dot(normed, w_query[...], preferred_element_type=F32).astype(BF16)
    query = query * jnp.asarray(HEAD_DIM**-0.5, BF16)
    rows = query.shape[0]
    lane = lax.broadcasted_iota(jnp.int32, (rows, 2 * HEAD_DIM), 1)
    for pair in range(PAIRS):
        both = query[:, 2 * HEAD_DIM * pair : 2 * HEAD_DIM * (pair + 1)]
        zero = jnp.zeros_like(both)
        query_ref[pair, :rows, :] = jnp.where(lane < HEAD_DIM, both, zero)
        query_ref[pair, rows:, :] = jnp.where(lane >= HEAD_DIM, both, zero)


def attend(normed, flags, w_key, w_value_t, query_ref, key_ref, value_ref, old, new):
    blocks = len(flags)
    rows = normed.shape[0] // blocks
    peak_ref, total_ref, numer_ref = new

    def span_of(pair):
        return slice(2 * HEAD_DIM * pair, 2 * HEAD_DIM * (pair + 1))

    def scores_of(pair):
        return lax.dot_general(
            key_ref[:, span_of(pair)], query_ref[pair], BY_ROWS, preferred_element_type=F32
        )

    def soften(pair, scores):
        line = slice(pair, pair + 1)
        parts = [scores[rows * b : rows * (b + 1)] for b in range(blocks)]
        peak = None if old is None else old[0][line, :]
        for flag, part in zip(flags, parts):
            top = jnp.max(part, axis=0, keepdims=True)
            if flag is not None:
                top = jnp.where(flag, top, -jnp.inf)
            peak = top if peak is None else jnp.maximum(peak, top)
        total = None
        weights = []
        for flag, part in zip(flags, parts):
            shift = peak if flag is None else jnp.where(flag, peak, jnp.inf)
            e = jnp.exp(part - shift)
            weights.append(e.astype(BF16))
            summed = jnp.sum(e, axis=0, keepdims=True)
            total = summed if total is None else total + summed
        keep = None
        if old is not None:
            keep = jnp.exp(old[0][line, :] - peak)
            total = old[1][line, :] * keep + total
        peak_ref[line, :] = peak
        total_ref[line, :] = total
        return (jnp.concatenate(weights, axis=0) if blocks > 1 else weights[0]), keep

    def gather_values(pair, weights, keep):
        span = span_of(pair)
        numer = jnp.dot(value_ref[span, :], weights, preferred_element_type=F32)
        for j in range(2):
            head = slice(span.start + HEAD_DIM * j, span.start + HEAD_DIM * (j + 1))
            lanes = slice(rows * j, rows * (j + 1))
            part = numer[HEAD_DIM * j : HEAD_DIM * (j + 1), lanes]
            if keep is not None:
                part = old[2][head, :] * keep[:, lanes] + part
            numer_ref[head, :] = part

    def project(group):
        span = slice(2 * HEAD_DIM * GROUP * group, 2 * HEAD_DIM * GROUP * (group + 1))
        key_ref[:, span] = jnp.dot(normed, w_key[:, span], preferred_element_type=F32).astype(BF16)
        value_ref[span, :] = lax.dot_general(
            w_value_t[span, :], normed, BY_ROWS, preferred_element_type=F32
        ).astype(BF16)

    project(0)
    scores = scores_of(0)
    held = None
    for pair in range(PAIRS):
        if pair % GROUP == 0 and pair + GROUP < PAIRS:
            project(pair // GROUP + 1)
        ahead = scores_of(pair + 1) if pair + 1 < PAIRS else None
        if held is not None:
            gather_values(pair - 1, *held)
        held = soften(pair, scores)
        scores = ahead
    gather_values(PAIRS - 1, *held)


def finish(total_ref, numer_ref, gain_col, w_out, source, headed_ref):
    rows = source.shape[0]
    for pair in range(PAIRS):
        for j in range(2):
            head = slice((2 * pair + j) * HEAD_DIM, (2 * pair + j + 1) * HEAD_DIM)
            attended = numer_ref[head, :] * (1.0 / total_ref[pair : pair + 1, rows * j : rows * (j + 1)])
            mean_sq = jnp.mean(attended * attended, axis=0, keepdims=True)
            headed_ref[head, :] = (attended * lax.rsqrt(mean_sq + 1e-06) * gain_col[head, :]).astype(BF16)
    update = lax.dot_general(headed_ref[...], w_out[...], BY_COLUMNS, preferred_element_type=F32)
    return (source.astype(F32) + update).astype(BF16)


def join_normed(block_refs, gain_ref):
    parts = [normalize(block[...], gain_ref[...]) for block in block_refs]
    return jnp.concatenate(parts, axis=0) if len(parts) > 1 else parts[0]


def listed(owners, slots, covis_list, covis_count):
    ids = owners(lax.axis_index("views"))
    count = covis_count[0]
    entries = [jnp.where(i < count, covis_list[0, i], -1) for i in range(covis_list.shape[1])]
    return [functools.reduce(jnp.logical_or, [entry == ids[s] for entry in entries]) for s in slots]


def first_kernel(
    owners, slots, own, other, covis_list, covis_count, in_gain, w_query, w_key, w_value,
    query, peak, total, numer, w_key_here, w_value_t,
    own_here, in_gain_here, w_query_here, w_value_here, key, value, arrived,
):
    copies = [
        pltpu.make_async_copy(source, target, arrived.at[i])
        for i, (source, target) in enumerate(
            (
                (own, own_here),
                (in_gain, in_gain_here),
                (w_query, w_query_here),
                (w_value, w_value_here),
                (w_key, w_key_here),
            )
        )
    ]
    for copy in copies:
        copy.start()
    flags = [None] + listed(owners, slots, covis_list, covis_count)
    copies[0].wait()
    copies[1].wait()
    normed = join_normed((own_here, other), in_gain_here)
    copies[2].wait()
    project_query(normed[: own.shape[0]], w_query_here, query)
    copies[3].wait()
    w_value_t[...] = w_value_here[...].T
    copies[4].wait()
    attend(normed, flags, w_key_here, w_value_t, query, key, value, None, (peak, total, numer))


def later_kernel(slots, owners, *refs):
    blocks = refs[: len(slots)]
    covis_list, covis_count, in_gain, w_key, w_value_t, query, peak, total, numer = refs[len(slots) : len(slots) + 9]
    new_peak, new_total, new_numer, key, value = refs[len(slots) + 9 :]
    attend(
        join_normed(blocks, in_gain), listed(owners, slots, covis_list, covis_count),
        w_key, w_value_t, query, key, value,
        (peak, total, numer), (new_peak, new_total, new_numer),
    )


def last_kernel(slots, owners, *refs):
    blocks = refs[: len(slots)]
    covis_list, covis_count, in_gain, w_key, w_value_t, query, peak, total, numer = refs[len(slots) : len(slots) + 9]
    out_gain, w_out, source, out = refs[len(slots) + 9 : len(slots) + 13]
    new_peak, new_total, new_numer, headed, w_out_here, source_here, arrived, key, value = refs[len(slots) + 13 :]
    copies = [
        pltpu.make_async_copy(w_out, w_out_here, arrived.at[0]),
        pltpu.make_async_copy(source, source_here, arrived.at[1]),
    ]
    for copy in copies:
        copy.start()
    attend(
        join_normed(blocks, in_gain), listed(owners, slots, covis_list, covis_count),
        w_key, w_value_t, query, key, value,
        (peak, total, numer), (new_peak, new_total, new_numer),
    )
    for copy in copies:
        copy.wait()
    out[...] = finish(new_total, new_numer, out_gain, w_out_here, source_here[...], headed)


VMEM = pl.BlockSpec(memory_space=pltpu.VMEM)
SMEM = pl.BlockSpec(memory_space=pltpu.SMEM)
HBM = pl.BlockSpec(memory_space=pltpu.HBM)


def scratch_for(blocks, rows, width):
    return [pltpu.VMEM((blocks * rows, width), BF16), pltpu.VMEM((width, blocks * rows), BF16)]


def in_hbm(array):
    return pltpu.with_memory_space_constraint(array, pltpu.HBM)


def tie(block, *done):
    return lax.optimization_barrier((block, *done))[0]


def routes(axis, view_count):
    def swap(mask):
        return lambda block: lax.ppermute(block, axis, [(i, i ^ mask) for i in range(view_count)])

    def shift(step):
        return lambda block: lax.ppermute(
            block, axis, [(i, (i + step) % view_count) for i in range(view_count)]
        )

    masks = (1, 2, 4, 10, 3, 5, 6, 11, 7, 12, 14, 13, 15)
    reached = all(
        v == (v + d) % view_count or any(v ^ mask == (v + d) % view_count for mask in masks)
        for v in range(view_count)
        for d in range(-REACH, REACH + 1)
    )
    if reached and max(masks) < view_count:

        def first(own):
            return {0: own} | {mask: swap(mask)(own) for mask in (10, 4, 2, 1)}

        def second(got, after):
            got[12] = swap(6)(after(got[10]))
            got[14] = swap(4)(after(got[10]))
            got[6] = swap(2)(after(got[4]))
            for mask in (4, 2):
                got[mask ^ 1] = swap(1)(after(got[mask]))

        def third(got, after):
            for mask in (10, 6):
                got[mask ^ 1] = swap(1)(after(got[mask]))

        def fourth(got, after):
            for mask in (14, 12):
                got[mask ^ 1] = swap(1)(after(got[mask]))

        return first, second, third, fourth, masks, lambda me: {mask: me ^ mask for mask in masks}

    hops = (REACH + 1) // 2
    names = ["partner"] + [(way, hop, side) for hop in range(1, hops + 1) for side in (0, 1) for way in (2, -2)]

    def first(own):
        got = {"partner": swap(1)(own)}
        for way in (2, -2):
            got[way, 1, 0] = shift(way)(own)
        return got

    def second(got, after):
        for way in (2, -2):
            for hop in range(2, hops + 1):
                got[way, hop, 0] = shift(way)(after(got[way, hop - 1, 0]))
            got[way, 1, 1] = swap(1)(after(got[way, 1, 0]))

    def third(got, after):
        for way in (2, -2):
            got[way, 2, 1] = swap(1)(after(got[way, 2, 0]))

    def fourth(got, after):
        for way in (2, -2):
            for hop in range(3, hops + 1):
                got[way, hop, 1] = swap(1)(after(got[way, hop, 0]))

    def owners(me):
        ids = {"partner": me ^ 1}
        for way in (2, -2):
            for hop in range(1, hops + 1):
                far = lax.rem(me - way * hop + view_count, view_count)
                ids[way, hop, 0] = far
                ids[way, hop, 1] = far ^ 1
        return ids

    return first, second, third, fourth, names, owners


def cost_of(blocks, rows, width, weight):
    keys = int(blocks * rows * weight)
    return pl.CostEstimate(
        flops=4 * keys * width * width + 8 * keys * rows * width,
        bytes_accessed=2 * blocks * rows * width,
        transcendentals=0,
    )


def on_device(view_count, tokens, in_gain, w_query, w_key, w_value, w_out, out_gain, covis_list, covis_count):
    source = tokens[0]
    rows, width = source.shape
    first, second, third, fourth, names, owners = routes("views", view_count)
    gain_row = in_gain.reshape(1, width)
    gain_col = out_gain.reshape(width, 1)
    pair_rows = 2 * rows
    state_shapes = [
        pltpu.VMEM((PAIRS, pair_rows), F32),
        pltpu.VMEM((PAIRS, pair_rows), F32),
        pltpu.VMEM((width, rows), F32),
    ]
    params = pltpu.CompilerParams(vmem_limit_bytes=24 * MIB)

    slots_done = []

    def call_later(got, slots, state, tail=None):
        slots_done.append(slots)
        count = len(slots)
        held = [
            pltpu.with_memory_space_constraint(x, pltpu.VMEM) for x in (w_key_here, w_value_t, query, *state)
        ]
        parts = [got[s] for s in slots] + [covis_list, covis_count, gain_row] + held
        specs = [VMEM] * count + [SMEM] * 2 + [VMEM] * 7
        scratch = scratch_for(count, rows, width)
        if tail is None:
            return pl.pallas_call(
                functools.partial(later_kernel, slots, owners),
                out_shape=state_shapes,
                in_specs=specs,
                out_specs=[VMEM] * 3,
                scratch_shapes=scratch,
                compiler_params=params,
                cost_estimate=cost_of(count, rows, width, WEIGHT[len(slots_done)]),
            )(*parts)
        return pl.pallas_call(
            functools.partial(last_kernel, slots, owners),
            out_shape=jax.ShapeDtypeStruct((rows, width), BF16),
            in_specs=specs + [VMEM, HBM, HBM],
            out_specs=VMEM,
            scratch_shapes=state_shapes
            + [pltpu.VMEM((width, rows), BF16), pltpu.VMEM(w_out.shape, BF16)]
            + [pltpu.VMEM(source.shape, BF16), pltpu.SemaphoreType.DMA((2,))]
            + scratch,
            compiler_params=params,
            cost_estimate=cost_of(count, rows, width, WEIGHT[len(slots_done)]),
        )(*parts, *tail)

    got = first(source)
    query, *state, w_key_here, w_value_t = pl.pallas_call(
        functools.partial(first_kernel, owners, names[:1]),
        out_shape=[pltpu.VMEM((PAIRS, pair_rows, 2 * HEAD_DIM), BF16)]
        + state_shapes
        + [pltpu.VMEM(w_key.shape, BF16), pltpu.VMEM(w_value.shape, BF16)],
        in_specs=[HBM, VMEM, SMEM, SMEM, HBM, HBM, HBM, HBM],
        out_specs=[VMEM] * 6,
        scratch_shapes=[
            pltpu.VMEM(source.shape, BF16),
            pltpu.VMEM(gain_row.shape, F32),
            pltpu.VMEM(w_query.shape, BF16),
            pltpu.VMEM(w_value.shape, BF16),
        ]
        + scratch_for(2, rows, width)
        + [pltpu.SemaphoreType.DMA((5,))],
        compiler_params=params,
        cost_estimate=cost_of(2, rows, width, WEIGHT[0]),
    )(
        in_hbm(source), got[names[0]], covis_list, covis_count,
        *map(in_hbm, (gain_row, w_query, w_key, w_value)),
    )
    for wave, slots in (
        (second, names[1:4]),
        (third, names[4:7]),
        (None, names[7:9]),
        (fourth, names[9:11]),
    ):
        if wave is not None:
            mark = state[0]
            wave(got, lambda block: tie(block, mark))
        state = call_later(got, slots, state)
    return call_later(got, names[11:], state, (gain_col, in_hbm(w_out), in_hbm(source)))[None]


def solution(mesh):
    in_specs = (
        P(("groups", "views"), None, None),
        P(),
        P(),
        P(),
        P(),
        P(),
        P(),
        P(("groups", "views"), None),
        P(("groups", "views")),
    )
    out_specs = P(("groups", "views"), None, None)
    return jax.shard_map(
        functools.partial(on_device, mesh.shape["views"]),
        mesh=mesh, in_specs=in_specs, out_specs=out_specs, check_vma=False,
    )
```

```python
import functools

import jax
import jax.numpy as jnp
from jax import lax
from jax.experimental import pallas as pl
from jax.experimental.pallas import tpu as pltpu
from jax.sharding import PartitionSpec as P

HEADS = 16
HEAD_DIM = 64
REACH = 6
PAIRS = HEADS // 2
GROUP = 4
WEIGHT = (3, 3, 3, 3, 3, 3)
F32 = jnp.float32
BF16 = jnp.bfloat16
BY_ROWS = (((1,), (1,)), ((), ()))
BY_COLUMNS = (((0,), (0,)), ((), ()))
MIB = 1024 * 1024


def normalize(block, gain):
    values = block.astype(F32)
    mean_sq = jnp.mean(values * values, axis=-1, keepdims=True)
    return (values * lax.rsqrt(mean_sq + 1e-06) * gain).astype(BF16)


def project_query(normed, w_query, query_ref):
    query = jnp.dot(normed, w_query[...], preferred_element_type=F32).astype(BF16)
    query = query * jnp.asarray(HEAD_DIM**-0.5, BF16)
    rows = query.shape[0]
    lane = lax.broadcasted_iota(jnp.int32, (rows, 2 * HEAD_DIM), 1)
    for pair in range(PAIRS):
        both = query[:, 2 * HEAD_DIM * pair : 2 * HEAD_DIM * (pair + 1)]
        zero = jnp.zeros_like(both)
        query_ref[pair, :rows, :] = jnp.where(lane < HEAD_DIM, both, zero)
        query_ref[pair, rows:, :] = jnp.where(lane >= HEAD_DIM, both, zero)


def attend(normed, flags, w_key, w_value_t, query_ref, key_ref, value_ref, old, new, after_pair=None):
    blocks = len(flags)
    rows = normed.shape[0] // blocks
    peak_ref, total_ref, numer_ref = new

    def span_of(pair):
        return slice(2 * HEAD_DIM * pair, 2 * HEAD_DIM * (pair + 1))

    def scores_of(pair):
        return lax.dot_general(
            key_ref[:, span_of(pair)], query_ref[pair], BY_ROWS, preferred_element_type=F32
        )

    def soften(pair, scores):
        line = slice(pair, pair + 1)
        parts = [scores[rows * b : rows * (b + 1)] for b in range(blocks)]
        peak = None if old is None else old[0][line, :]
        for flag, part in zip(flags, parts):
            top = jnp.max(part, axis=0, keepdims=True)
            if flag is not None:
                top = jnp.where(flag, top, -jnp.inf)
            peak = top if peak is None else jnp.maximum(peak, top)
        total = None
        weights = []
        for flag, part in zip(flags, parts):
            shift = peak if flag is None else jnp.where(flag, peak, jnp.inf)
            e = jnp.exp(part - shift)
            weights.append(e.astype(BF16))
            summed = jnp.sum(e, axis=0, keepdims=True)
            total = summed if total is None else total + summed
        keep = None
        if old is not None:
            keep = jnp.exp(old[0][line, :] - peak)
            total = old[1][line, :] * keep + total
        peak_ref[line, :] = peak
        total_ref[line, :] = total
        return (jnp.concatenate(weights, axis=0) if blocks > 1 else weights[0]), keep

    def gather_values(pair, weights, keep):
        span = span_of(pair)
        numer = jnp.dot(value_ref[span, :], weights, preferred_element_type=F32)
        for j in range(2):
            head = slice(span.start + HEAD_DIM * j, span.start + HEAD_DIM * (j + 1))
            lanes = slice(rows * j, rows * (j + 1))
            part = numer[HEAD_DIM * j : HEAD_DIM * (j + 1), lanes]
            if keep is not None:
                part = old[2][head, :] * keep[:, lanes] + part
            if after_pair is None:
                numer_ref[head, :] = part
            else:
                after_pair(pair, head, lanes, part)

    def project(group):
        span = slice(2 * HEAD_DIM * GROUP * group, 2 * HEAD_DIM * GROUP * (group + 1))
        key_ref[:, span] = jnp.dot(normed, w_key[:, span], preferred_element_type=F32).astype(BF16)
        value_ref[span, :] = lax.dot_general(
            w_value_t[span, :], normed, BY_ROWS, preferred_element_type=F32
        ).astype(BF16)

    project(0)
    scores = scores_of(0)
    held = None
    for pair in range(PAIRS):
        if pair % GROUP == 0 and pair + GROUP < PAIRS:
            project(pair // GROUP + 1)
        ahead = scores_of(pair + 1) if pair + 1 < PAIRS else None
        if held is not None:
            gather_values(pair - 1, *held)
        held = soften(pair, scores)
        scores = ahead
    gather_values(PAIRS - 1, *held)


def finish_head(total_ref, gain_col, headed_ref, pair, head, lanes, numer):
    attended = numer * (1.0 / total_ref[pair : pair + 1, lanes])
    mean_sq = jnp.mean(attended * attended, axis=0, keepdims=True)
    headed_ref[head, :] = (attended * lax.rsqrt(mean_sq + 1e-06) * gain_col[head, :]).astype(BF16)


def mix(headed_ref, w_out, source):
    update = lax.dot_general(headed_ref[...], w_out[...], BY_COLUMNS, preferred_element_type=F32)
    return (source.astype(F32) + update).astype(BF16)


def join_normed(block_refs, gain_ref):
    parts = [normalize(block[...], gain_ref[...]) for block in block_refs]
    return jnp.concatenate(parts, axis=0) if len(parts) > 1 else parts[0]


def listed(owners, slots, covis_list, covis_count):
    ids = owners(lax.axis_index("views"))
    count = covis_count[0]
    entries = [jnp.where(i < count, covis_list[0, i], -1) for i in range(covis_list.shape[1])]
    return [functools.reduce(jnp.logical_or, [entry == ids[s] for entry in entries]) for s in slots]


def first_kernel(
    owners, slots, own, other, covis_list, covis_count, in_gain, w_query, w_key, w_value,
    query, peak, total, numer, w_key_here, w_value_t,
    own_here, in_gain_here, w_query_here, w_value_here, key, value, arrived,
):
    copies = [
        pltpu.make_async_copy(source, target, arrived.at[i])
        for i, (source, target) in enumerate(
            (
                (own, own_here),
                (in_gain, in_gain_here),
                (w_query, w_query_here),
                (w_value, w_value_here),
                (w_key, w_key_here),
            )
        )
    ]
    for copy in copies:
        copy.start()
    flags = [None] + listed(owners, slots, covis_list, covis_count)
    copies[0].wait()
    copies[1].wait()
    normed = join_normed((own_here, other), in_gain_here)
    copies[2].wait()
    project_query(normed[: own.shape[0]], w_query_here, query)
    copies[3].wait()
    w_value_t[...] = w_value_here[...].T
    copies[4].wait()
    attend(normed, flags, w_key_here, w_value_t, query, key, value, None, (peak, total, numer))


def later_kernel(slots, owners, *refs):
    blocks = refs[: len(slots)]
    covis_list, covis_count, in_gain, w_key, w_value_t, query, peak, total, numer = refs[len(slots) : len(slots) + 9]
    new_peak, new_total, new_numer, key, value = refs[len(slots) + 9 :]
    attend(
        join_normed(blocks, in_gain), listed(owners, slots, covis_list, covis_count),
        w_key, w_value_t, query, key, value,
        (peak, total, numer), (new_peak, new_total, new_numer),
    )


def last_kernel(slots, owners, *refs):
    blocks = refs[: len(slots)]
    covis_list, covis_count, in_gain, w_key, w_value_t, query, peak, total, numer = refs[len(slots) : len(slots) + 9]
    out_gain, w_out, source, out = refs[len(slots) + 9 : len(slots) + 13]
    new_peak, new_total, headed, w_out_here, source_here, arrived, key, value = refs[len(slots) + 13 :]
    copies = [
        pltpu.make_async_copy(w_out, w_out_here, arrived.at[0]),
        pltpu.make_async_copy(source, source_here, arrived.at[1]),
    ]
    for copy in copies:
        copy.start()
    attend(
        join_normed(blocks, in_gain), listed(owners, slots, covis_list, covis_count),
        w_key, w_value_t, query, key, value,
        (peak, total, numer), (new_peak, new_total, None),
        functools.partial(finish_head, new_total, out_gain, headed),
    )
    for copy in copies:
        copy.wait()
    out[...] = mix(headed, w_out_here, source_here[...])


VMEM = pl.BlockSpec(memory_space=pltpu.VMEM)
SMEM = pl.BlockSpec(memory_space=pltpu.SMEM)
HBM = pl.BlockSpec(memory_space=pltpu.HBM)


def scratch_for(blocks, rows, width):
    return [pltpu.VMEM((blocks * rows, width), BF16), pltpu.VMEM((width, blocks * rows), BF16)]


def in_hbm(array):
    return pltpu.with_memory_space_constraint(array, pltpu.HBM)


def tie(block, *done):
    return lax.optimization_barrier((block, *done))[0]


def routes(axis, view_count):
    def swap(mask):
        return lambda block: lax.ppermute(block, axis, [(i, i ^ mask) for i in range(view_count)])

    def shift(step):
        return lambda block: lax.ppermute(
            block, axis, [(i, (i + step) % view_count) for i in range(view_count)]
        )

    masks = (1, 2, 4, 10, 3, 5, 6, 11, 7, 12, 14, 13, 15)
    reached = all(
        v == (v + d) % view_count or any(v ^ mask == (v + d) % view_count for mask in masks)
        for v in range(view_count)
        for d in range(-REACH, REACH + 1)
    )
    if reached and max(masks) < view_count:

        def first(own):
            return {0: own} | {mask: swap(mask)(own) for mask in (10, 4, 2, 1)}

        def second(got, after):
            got[12] = swap(6)(after(got[10]))
            got[14] = swap(4)(after(got[10]))
            got[6] = swap(2)(after(got[4]))
            for mask in (4, 2):
                got[mask ^ 1] = swap(1)(after(got[mask]))

        def third(got, after):
            for mask in (10, 6):
                got[mask ^ 1] = swap(1)(after(got[mask]))

        def fourth(got, after):
            for mask in (14, 12):
                got[mask ^ 1] = swap(1)(after(got[mask]))

        return first, second, third, fourth, masks, lambda me: {mask: me ^ mask for mask in masks}

    hops = (REACH + 1) // 2
    names = ["partner"] + [(way, hop, side) for hop in range(1, hops + 1) for side in (0, 1) for way in (2, -2)]

    def first(own):
        got = {"partner": swap(1)(own)}
        for way in (2, -2):
            got[way, 1, 0] = shift(way)(own)
        return got

    def second(got, after):
        for way in (2, -2):
            for hop in range(2, hops + 1):
                got[way, hop, 0] = shift(way)(after(got[way, hop - 1, 0]))
            got[way, 1, 1] = swap(1)(after(got[way, 1, 0]))

    def third(got, after):
        for way in (2, -2):
            got[way, 2, 1] = swap(1)(after(got[way, 2, 0]))

    def fourth(got, after):
        for way in (2, -2):
            for hop in range(3, hops + 1):
                got[way, hop, 1] = swap(1)(after(got[way, hop, 0]))

    def owners(me):
        ids = {"partner": me ^ 1}
        for way in (2, -2):
            for hop in range(1, hops + 1):
                far = lax.rem(me - way * hop + view_count, view_count)
                ids[way, hop, 0] = far
                ids[way, hop, 1] = far ^ 1
        return ids

    return first, second, third, fourth, names, owners


def cost_of(blocks, rows, width, weight):
    keys = int(blocks * rows * weight)
    return pl.CostEstimate(
        flops=4 * keys * width * width + 8 * keys * rows * width,
        bytes_accessed=2 * blocks * rows * width,
        transcendentals=0,
    )


def on_device(view_count, tokens, in_gain, w_query, w_key, w_value, w_out, out_gain, covis_list, covis_count):
    source = tokens[0]
    rows, width = source.shape
    first, second, third, fourth, names, owners = routes("views", view_count)
    gain_row = in_gain.reshape(1, width)
    gain_col = out_gain.reshape(width, 1)
    pair_rows = 2 * rows
    state_shapes = [
        pltpu.VMEM((PAIRS, pair_rows), F32),
        pltpu.VMEM((PAIRS, pair_rows), F32),
        pltpu.VMEM((width, rows), F32),
    ]
    params = pltpu.CompilerParams(vmem_limit_bytes=24 * MIB)

    slots_done = []

    def call_later(got, slots, state, tail=None):
        slots_done.append(slots)
        count = len(slots)
        held = [
            pltpu.with_memory_space_constraint(x, pltpu.VMEM) for x in (w_key_here, w_value_t, query, *state)
        ]
        parts = [got[s] for s in slots] + [covis_list, covis_count, gain_row] + held
        specs = [VMEM] * count + [SMEM] * 2 + [VMEM] * 7
        scratch = scratch_for(count, rows, width)
        if tail is None:
            return pl.pallas_call(
                functools.partial(later_kernel, slots, owners),
                out_shape=state_shapes,
                in_specs=specs,
                out_specs=[VMEM] * 3,
                scratch_shapes=scratch,
                compiler_params=params,
                cost_estimate=cost_of(count, rows, width, WEIGHT[len(slots_done)]),
            )(*parts)
        return pl.pallas_call(
            functools.partial(last_kernel, slots, owners),
            out_shape=jax.ShapeDtypeStruct((rows, width), BF16),
            in_specs=specs + [VMEM, HBM, HBM],
            out_specs=VMEM,
            scratch_shapes=state_shapes[:2]
            + [pltpu.VMEM((width, rows), BF16), pltpu.VMEM(w_out.shape, BF16)]
            + [pltpu.VMEM(source.shape, BF16), pltpu.SemaphoreType.DMA((2,))]
            + scratch,
            compiler_params=params,
            cost_estimate=cost_of(count, rows, width, WEIGHT[len(slots_done)]),
        )(*parts, *tail)

    got = first(source)
    query, *state, w_key_here, w_value_t = pl.pallas_call(
        functools.partial(first_kernel, owners, names[:1]),
        out_shape=[pltpu.VMEM((PAIRS, pair_rows, 2 * HEAD_DIM), BF16)]
        + state_shapes
        + [pltpu.VMEM(w_key.shape, BF16), pltpu.VMEM(w_value.shape, BF16)],
        in_specs=[HBM, VMEM, SMEM, SMEM, HBM, HBM, HBM, HBM],
        out_specs=[VMEM] * 6,
        scratch_shapes=[
            pltpu.VMEM(source.shape, BF16),
            pltpu.VMEM(gain_row.shape, F32),
            pltpu.VMEM(w_query.shape, BF16),
            pltpu.VMEM(w_value.shape, BF16),
        ]
        + scratch_for(2, rows, width)
        + [pltpu.SemaphoreType.DMA((5,))],
        compiler_params=params,
        cost_estimate=cost_of(2, rows, width, WEIGHT[0]),
    )(
        in_hbm(source), got[names[0]], covis_list, covis_count,
        *map(in_hbm, (gain_row, w_query, w_key, w_value)),
    )
    for wave, slots in (
        (second, names[1:4]),
        (third, names[4:7]),
        (None, names[7:9]),
        (fourth, names[9:11]),
    ):
        if wave is not None:
            mark = state[0]
            wave(got, lambda block: tie(block, mark))
        state = call_later(got, slots, state)
    return call_later(got, names[11:], state, (gain_col, in_hbm(w_out), in_hbm(source)))[None]


def solution(mesh):
    in_specs = (
        P(("groups", "views"), None, None),
        P(),
        P(),
        P(),
        P(),
        P(),
        P(),
        P(("groups", "views"), None),
        P(("groups", "views")),
    )
    out_specs = P(("groups", "views"), None, None)
    return jax.shard_map(
        functools.partial(on_device, mesh.shape["views"]),
        mesh=mesh, in_specs=in_specs, out_specs=out_specs, check_vma=False,
    )
```

```python
import functools

import jax
import jax.numpy as jnp
from jax import lax
from jax.experimental import pallas as pl
from jax.experimental.pallas import tpu as pltpu
from jax.sharding import PartitionSpec as P

HEADS = 16
HEAD_DIM = 64
REACH = 6
PAIRS = HEADS // 2
GROUP = 4
WEIGHT = (3, 3, 3, 3, 3, 3)
F32 = jnp.float32
BF16 = jnp.bfloat16
BY_ROWS = (((1,), (1,)), ((), ()))
BY_COLUMNS = (((0,), (0,)), ((), ()))
MIB = 1024 * 1024


def normalize(block, gain):
    values = block.astype(F32)
    mean_sq = jnp.mean(values * values, axis=-1, keepdims=True)
    return (values * lax.rsqrt(mean_sq + 1e-06) * gain).astype(BF16)


def project_query(normed, w_query, query_ref):
    query = jnp.dot(normed, w_query[...], preferred_element_type=F32).astype(BF16)
    query = query * jnp.asarray(HEAD_DIM**-0.5, BF16)
    rows = query.shape[0]
    lane = lax.broadcasted_iota(jnp.int32, (rows, 2 * HEAD_DIM), 1)
    for pair in range(PAIRS):
        both = query[:, 2 * HEAD_DIM * pair : 2 * HEAD_DIM * (pair + 1)]
        zero = jnp.zeros_like(both)
        query_ref[pair, :rows, :] = jnp.where(lane < HEAD_DIM, both, zero)
        query_ref[pair, rows:, :] = jnp.where(lane >= HEAD_DIM, both, zero)


def attend(normed, flags, w_key, w_value_t, query_ref, key_ref, value_ref, old, new, after_pair=None):
    blocks = len(flags)
    rows = normed.shape[0] // blocks
    peak_ref, total_ref, numer_ref = new

    def span_of(pair):
        return slice(2 * HEAD_DIM * pair, 2 * HEAD_DIM * (pair + 1))

    def scores_of(pair):
        return lax.dot_general(
            key_ref[:, span_of(pair)], query_ref[pair], BY_ROWS, preferred_element_type=F32
        )

    def soften(pair, scores):
        line = slice(pair, pair + 1)
        parts = [scores[rows * b : rows * (b + 1)] for b in range(blocks)]
        peak = None if old is None else old[0][line, :]
        for flag, part in zip(flags, parts):
            top = jnp.max(part, axis=0, keepdims=True)
            if flag is not None:
                top = jnp.where(flag, top, -jnp.inf)
            peak = top if peak is None else jnp.maximum(peak, top)
        total = None
        weights = []
        for flag, part in zip(flags, parts):
            shift = peak if flag is None else jnp.where(flag, peak, jnp.inf)
            e = jnp.exp(part - shift)
            weights.append(e.astype(BF16))
            summed = jnp.sum(e, axis=0, keepdims=True)
            total = summed if total is None else total + summed
        keep = None
        if old is not None:
            keep = jnp.exp(old[0][line, :] - peak)
            total = old[1][line, :] * keep + total
        peak_ref[line, :] = peak
        total_ref[line, :] = total
        return (jnp.concatenate(weights, axis=0) if blocks > 1 else weights[0]), keep

    def gather_values(pair, weights, keep):
        span = span_of(pair)
        numer = jnp.dot(value_ref[span, :], weights, preferred_element_type=F32)
        for j in range(2):
            head = slice(span.start + HEAD_DIM * j, span.start + HEAD_DIM * (j + 1))
            lanes = slice(rows * j, rows * (j + 1))
            part = numer[HEAD_DIM * j : HEAD_DIM * (j + 1), lanes]
            if keep is not None:
                part = old[2][head, :] * keep[:, lanes] + part
            if after_pair is None:
                numer_ref[head, :] = part
            else:
                after_pair(pair, head, lanes, part)

    def project(group):
        span = slice(2 * HEAD_DIM * GROUP * group, 2 * HEAD_DIM * GROUP * (group + 1))
        key_ref[:, span] = jnp.dot(normed, w_key[:, span], preferred_element_type=F32).astype(BF16)
        value_ref[span, :] = lax.dot_general(
            w_value_t[span, :], normed, BY_ROWS, preferred_element_type=F32
        ).astype(BF16)

    project(0)
    scores = scores_of(0)
    held = None
    for pair in range(PAIRS):
        if pair % GROUP == 0 and pair + GROUP < PAIRS:
            project(pair // GROUP + 1)
        ahead = scores_of(pair + 1) if pair + 1 < PAIRS else None
        if held is not None:
            gather_values(pair - 1, *held)
        held = soften(pair, scores)
        scores = ahead
    gather_values(PAIRS - 1, *held)


def finish_head(total_ref, gain_col, headed_ref, pair, head, lanes, numer):
    attended = numer * (1.0 / total_ref[pair : pair + 1, lanes])
    mean_sq = jnp.mean(attended * attended, axis=0, keepdims=True)
    headed_ref[head, :] = (attended * lax.rsqrt(mean_sq + 1e-06) * gain_col[head, :]).astype(BF16)


def mix(headed_ref, w_out, source):
    update = lax.dot_general(headed_ref[...], w_out[...], BY_COLUMNS, preferred_element_type=F32)
    return (source.astype(F32) + update).astype(BF16)


def join_normed(block_refs, gain_ref):
    parts = [normalize(block[...], gain_ref[...]) for block in block_refs]
    return jnp.concatenate(parts, axis=0) if len(parts) > 1 else parts[0]


def listed(owners, slots, covis_list, covis_count):
    ids = owners(lax.axis_index("views"))
    count = covis_count[0]
    entries = [jnp.where(i < count, covis_list[0, i], -1) for i in range(covis_list.shape[1])]
    return [functools.reduce(jnp.logical_or, [entry == ids[s] for entry in entries]) for s in slots]


def first_kernel(
    owners, slots, own, other, covis_list, covis_count, in_gain, w_query, w_key, w_value,
    query, peak, total, numer, w_key_here, w_value_t,
    own_here, in_gain_here, w_query_here, w_value_here, key, value, arrived,
):
    copies = [
        pltpu.make_async_copy(source, target, arrived.at[i])
        for i, (source, target) in enumerate(
            (
                (own, own_here),
                (in_gain, in_gain_here),
                (w_query, w_query_here),
                (w_value, w_value_here),
                (w_key, w_key_here),
            )
        )
    ]
    for copy in copies:
        copy.start()
    flags = [None] + listed(owners, slots, covis_list, covis_count)
    copies[0].wait()
    copies[1].wait()
    normed = join_normed((own_here, other), in_gain_here)
    copies[2].wait()
    project_query(normed[: own.shape[0]], w_query_here, query)
    copies[3].wait()
    w_value_t[...] = w_value_here[...].T
    copies[4].wait()
    attend(normed, flags, w_key_here, w_value_t, query, key, value, None, (peak, total, numer))


def later_kernel(slots, owners, *refs):
    blocks = refs[: len(slots)]
    covis_list, covis_count, in_gain, w_key, w_value_t, query, peak, total, numer = refs[len(slots) : len(slots) + 9]
    new_peak, new_total, new_numer, key, value = refs[len(slots) + 9 :]
    attend(
        join_normed(blocks, in_gain), listed(owners, slots, covis_list, covis_count),
        w_key, w_value_t, query, key, value,
        (peak, total, numer), (new_peak, new_total, new_numer),
    )


def last_kernel(slots, owners, *refs):
    blocks = refs[: len(slots)]
    covis_list, covis_count, in_gain, w_key, w_value_t, query, peak, total, numer = refs[len(slots) : len(slots) + 9]
    out_gain, w_out, source, out = refs[len(slots) + 9 : len(slots) + 13]
    new_peak, new_total, headed, w_out_here, source_here, arrived, key, value = refs[len(slots) + 13 :]
    copies = [
        pltpu.make_async_copy(w_out, w_out_here, arrived.at[0]),
        pltpu.make_async_copy(source, source_here, arrived.at[1]),
    ]
    for copy in copies:
        copy.start()
    attend(
        join_normed(blocks, in_gain), listed(owners, slots, covis_list, covis_count),
        w_key, w_value_t, query, key, value,
        (peak, total, numer), (new_peak, new_total, None),
        functools.partial(finish_head, new_total, out_gain, headed),
    )
    for copy in copies:
        copy.wait()
    out[...] = mix(headed, w_out_here, source_here[...])


VMEM = pl.BlockSpec(memory_space=pltpu.VMEM)
SMEM = pl.BlockSpec(memory_space=pltpu.SMEM)
HBM = pl.BlockSpec(memory_space=pltpu.HBM)


def scratch_for(blocks, rows, width):
    return [pltpu.VMEM((blocks * rows, width), BF16), pltpu.VMEM((width, blocks * rows), BF16)]


def in_hbm(array):
    return pltpu.with_memory_space_constraint(array, pltpu.HBM)


def tie(block, *done):
    return lax.optimization_barrier((block, *done))[0]


def routes(axis, view_count):
    def swap(mask):
        return lambda block: lax.ppermute(block, axis, [(i, i ^ mask) for i in range(view_count)])

    def shift(step):
        return lambda block: lax.ppermute(
            block, axis, [(i, (i + step) % view_count) for i in range(view_count)]
        )

    masks = (1, 2, 4, 10, 3, 5, 6, 11, 7, 12, 14, 13, 15)
    reached = all(
        v == (v + d) % view_count or any(v ^ mask == (v + d) % view_count for mask in masks)
        for v in range(view_count)
        for d in range(-REACH, REACH + 1)
    )
    if reached and max(masks) < view_count:

        def first(own):
            return {0: own} | {mask: swap(mask)(own) for mask in (10, 4, 2, 1)}

        def second(got, after):
            got[12] = swap(6)(after(got[10]))
            got[14] = swap(4)(after(got[10]))
            got[6] = swap(2)(after(got[4]))
            got[5] = swap(1)(after(got[4]))
            got[3] = swap(1)(tie(after(got[2]), got[4]))

        def third(got, after):
            for mask in (10, 6):
                got[mask ^ 1] = swap(1)(after(got[mask]))

        def fourth(got, after):
            for mask in (14, 12):
                got[mask ^ 1] = swap(1)(after(got[mask]))

        return first, second, third, fourth, masks, lambda me: {mask: me ^ mask for mask in masks}

    hops = (REACH + 1) // 2
    names = ["partner"] + [(way, hop, side) for hop in range(1, hops + 1) for side in (0, 1) for way in (2, -2)]

    def first(own):
        got = {"partner": swap(1)(own)}
        for way in (2, -2):
            got[way, 1, 0] = shift(way)(own)
        return got

    def second(got, after):
        for way in (2, -2):
            for hop in range(2, hops + 1):
                got[way, hop, 0] = shift(way)(after(got[way, hop - 1, 0]))
            got[way, 1, 1] = swap(1)(after(got[way, 1, 0]))

    def third(got, after):
        for way in (2, -2):
            got[way, 2, 1] = swap(1)(after(got[way, 2, 0]))

    def fourth(got, after):
        for way in (2, -2):
            for hop in range(3, hops + 1):
                got[way, hop, 1] = swap(1)(after(got[way, hop, 0]))

    def owners(me):
        ids = {"partner": me ^ 1}
        for way in (2, -2):
            for hop in range(1, hops + 1):
                far = lax.rem(me - way * hop + view_count, view_count)
                ids[way, hop, 0] = far
                ids[way, hop, 1] = far ^ 1
        return ids

    return first, second, third, fourth, names, owners


def cost_of(blocks, rows, width, weight):
    keys = int(blocks * rows * weight)
    return pl.CostEstimate(
        flops=4 * keys * width * width + 8 * keys * rows * width,
        bytes_accessed=2 * blocks * rows * width,
        transcendentals=0,
    )


def on_device(view_count, tokens, in_gain, w_query, w_key, w_value, w_out, out_gain, covis_list, covis_count):
    source = tokens[0]
    rows, width = source.shape
    first, second, third, fourth, names, owners = routes("views", view_count)
    gain_row = in_gain.reshape(1, width)
    gain_col = out_gain.reshape(width, 1)
    pair_rows = 2 * rows
    state_shapes = [
        pltpu.VMEM((PAIRS, pair_rows), F32),
        pltpu.VMEM((PAIRS, pair_rows), F32),
        pltpu.VMEM((width, rows), F32),
    ]
    params = pltpu.CompilerParams(vmem_limit_bytes=24 * MIB)

    slots_done = []

    def call_later(got, slots, state, tail=None):
        slots_done.append(slots)
        count = len(slots)
        held = [
            pltpu.with_memory_space_constraint(x, pltpu.VMEM) for x in (w_key_here, w_value_t, query, *state)
        ]
        parts = [got[s] for s in slots] + [covis_list, covis_count, gain_row] + held
        specs = [VMEM] * count + [SMEM] * 2 + [VMEM] * 7
        scratch = scratch_for(count, rows, width)
        if tail is None:
            return pl.pallas_call(
                functools.partial(later_kernel, slots, owners),
                out_shape=state_shapes,
                in_specs=specs,
                out_specs=[VMEM] * 3,
                scratch_shapes=scratch,
                compiler_params=params,
                cost_estimate=cost_of(count, rows, width, WEIGHT[len(slots_done)]),
            )(*parts)
        return pl.pallas_call(
            functools.partial(last_kernel, slots, owners),
            out_shape=jax.ShapeDtypeStruct((rows, width), BF16),
            in_specs=specs + [VMEM, HBM, HBM],
            out_specs=VMEM,
            scratch_shapes=state_shapes[:2]
            + [pltpu.VMEM((width, rows), BF16), pltpu.VMEM(w_out.shape, BF16)]
            + [pltpu.VMEM(source.shape, BF16), pltpu.SemaphoreType.DMA((2,))]
            + scratch,
            compiler_params=params,
            cost_estimate=cost_of(count, rows, width, WEIGHT[len(slots_done)]),
        )(*parts, *tail)

    got = first(source)
    query, *state, w_key_here, w_value_t = pl.pallas_call(
        functools.partial(first_kernel, owners, names[:1]),
        out_shape=[pltpu.VMEM((PAIRS, pair_rows, 2 * HEAD_DIM), BF16)]
        + state_shapes
        + [pltpu.VMEM(w_key.shape, BF16), pltpu.VMEM(w_value.shape, BF16)],
        in_specs=[HBM, VMEM, SMEM, SMEM, HBM, HBM, HBM, HBM],
        out_specs=[VMEM] * 6,
        scratch_shapes=[
            pltpu.VMEM(source.shape, BF16),
            pltpu.VMEM(gain_row.shape, F32),
            pltpu.VMEM(w_query.shape, BF16),
            pltpu.VMEM(w_value.shape, BF16),
        ]
        + scratch_for(2, rows, width)
        + [pltpu.SemaphoreType.DMA((5,))],
        compiler_params=params,
        cost_estimate=cost_of(2, rows, width, WEIGHT[0]),
    )(
        in_hbm(source), got[names[0]], covis_list, covis_count,
        *map(in_hbm, (gain_row, w_query, w_key, w_value)),
    )
    for wave, slots in (
        (second, names[1:4]),
        (third, names[4:7]),
        (None, names[7:9]),
        (fourth, names[9:11]),
    ):
        if wave is not None:
            mark = state[0]
            wave(got, lambda block: tie(block, mark))
        state = call_later(got, slots, state)
    return call_later(got, names[11:], state, (gain_col, in_hbm(w_out), in_hbm(source)))[None]


def solution(mesh):
    in_specs = (
        P(("groups", "views"), None, None),
        P(),
        P(),
        P(),
        P(),
        P(),
        P(),
        P(("groups", "views"), None),
        P(("groups", "views")),
    )
    out_specs = P(("groups", "views"), None, None)
    return jax.shard_map(
        functools.partial(on_device, mesh.shape["views"]),
        mesh=mesh, in_specs=in_specs, out_specs=out_specs, check_vma=False,
    )
```
